32 devices in a mesh: groups: 2 (over y), rows: 4 (over z), heads: 4 (over x, core).
Axes of the slice: x: 2, y: 2, z: 4, core: 2. Of those that a mesh axis runs over, the one named last changes fastest.
Arguments:
- hidden: bfloat16 [2, 2048, 8192], P(None, ('groups', 'rows'), 'heads'), parts along dimension 1, may hold values from -6 to 6
- request_adapter: int32 [2048, 1], P(('groups', 'rows')), parts along dimension 0, may hold values from 0 to 3; in each aligned block of 256 rows (0 to 255, 256 to 511, ...) at most 128 rows name the same one
- adapter_row_index: int32 [4], replicated, may hold values from 0 to 3, each once
- adapter_scales: float32 [4], replicated, may hold values from 0.5 to 2
- down_weight_rows: bfloat16 [4, 128, 8192], P('rows', None, 'heads'), may hold values from -0.0625 to 0.0625
- query_up_weight: bfloat16 [4, 64, 8192], P('rows', None, 'heads'), may hold values from -0.75 to 0.75
- value_up_weight: bfloat16 [4, 64, 1024], P('rows', None, 'heads'), may hold values from -0.75 to 0.75
Outputs:
- delta_q: bfloat16 [2, 2048, 8192], P(None, ('groups', 'rows'), 'heads'), parts along dimension 1
- delta_v: bfloat16 [2, 2048, 1024], P(None, ('groups', 'rows'), 'heads'), parts along dimension 1
The draws below stay inside these ranges and needn't reach their ends.
There are 2 independent parts, one for each index of `groups`. The reference program is written for one: setup_inputs(seed, part) draws one part's arguments, and reference() takes and returns one part's arrays. A program takes and returns all parts, laid end to end along the dimension named above; an argument that names none is the same for every part. Nothing has to cross between parts.
Inputs may be any that keep to these rules, and one draw needn't show every extreme that they name: `request_adapter`: among the 256 requests of one device no adapter is named by more than 128 of them, a bound that some block reaches. `adapter_row_index`: each row of the adapter arrays holds exactly one adapter.
All inputs are finite; a program needn't handle non-finite values.
Results may differ from the reference program's by a relative error of at most 0.005.
Values may be sent and summed in bfloat16 or wider, within the bound.
A program may use at most 64 MiB of HBM per device.

```python
import math
import jax
import jax.numpy as jnp
import numpy as np
from jax import lax

MODEL_WIDTH = 8192
QUERY_WIDTH = 8192
VALUE_WIDTH = 1024
ADAPTER_RANK = 64
STEPS = 2
ROWS_DEV = 256
CAP = 128
REQ = 1024
ADAPTER_COUNT = 4
N_ROWS = 4


def steps_of(own_key, extent, cuts, low, high):
    factor_of, own = 1.0, jax.random.fold_in(own_key, 6)
    for axis_at, parts in cuts:
        steps = jnp.exp(jax.random.uniform(jax.random.fold_in(own, axis_at), (parts,), jnp.float32, low / len(cuts), high / len(cuts)))
        factor_of = factor_of * jnp.repeat(steps, extent[axis_at] // parts).reshape([-1 if axis == axis_at else 1 for axis in range(len(extent))])
    return factor_of


def shared_out(rng, own, number, rows, number_of, top, most, slope):
    order = jax.random.permutation(rng, number_of)
    packed, usual = portions_of(number_of, rows * top, most, slope, True), portions_of(number_of, rows * top, most, slope, False)
    places = jnp.arange(number_of)

    def named(sizes, rotation):
        used = int((sizes > 0).sum())
        fixed = max(1, used // 4)
        passed = fixed + (places - fixed + rotation * (used - fixed)) % max(1, number_of - fixed)
        return jnp.zeros((number_of,), jnp.int32).at[order[jnp.where(places < fixed, places, passed)]].set(jnp.asarray(sizes, jnp.int32))

    sizes = jnp.where(number % 4 == 0, named(packed, number // 4), named(usual, number - number // 4 - 1))
    mixed = jax.random.permutation(jax.random.fold_in(own, 3), number_of)
    giver, taker = mixed[0:number_of // 2 * 2:2], mixed[1:number_of // 2 * 2:2]
    slack = jnp.minimum(sizes[giver] - 1, most - sizes[taker]) // 2
    slack = jnp.where((giver == order[0]) | (taker == order[0]) | (sizes[taker] == 0), 0, jnp.maximum(slack, 0))
    passed = jax.random.randint(jax.random.fold_in(own, 4), (number_of // 2,), 0, 1 << 20) % (slack + 1)
    sizes = sizes.at[giver].add(-passed).at[taker].add(passed)
    members = jnp.searchsorted(jnp.cumsum(sizes), jnp.arange(rows * top), side="right").astype(jnp.int32)
    grid = members.reshape(top, rows).T
    grid = grid[jax.random.permutation(jax.random.fold_in(own, 1), rows)]
    rotation = jax.random.randint(jax.random.fold_in(own, 2), (rows, 1), 0, top)
    return jnp.take_along_axis(grid, (jnp.arange(top)[None, :] + rotation) % top, axis=1)


def portions_of(number_of, total, most, lean, full):
    portions = [(1 << 20) // math.isqrt(standing ** lean) + 1 for standing in range(1, number_of + 1)]
    largest = most if full else min(most, max(-(-total // number_of), total * portions[0] // sum(portions)))
    least = 1 if total - largest >= number_of - 1 else 0
    counts, spare = [largest] + [least] * (number_of - 1), total - largest - least * (number_of - 1)
    while spare > 0:
        free = [i for i in range(1, number_of) if counts[i] < largest] or [i for i in range(1, number_of) if counts[i] < most]
        mass, remaining = sum([portions[i] for i in free]), spare
        for i in free:
            extra = min(most - counts[i], max(1, remaining * portions[i] // mass), spare)
            counts[i] = counts[i] + extra
            spare = spare - extra
    return np.array(counts)


def bell_draw(own_key, dims, deviation, most, cuts=(), kind=jnp.bfloat16):
    result = jax.random.normal(own_key, dims, jnp.float32) * deviation
    if len(cuts) > 0:
        result = steps_of(own_key, dims, cuts, -0.22, 0.18) * result
    return jnp.clip(result, min=-most, max=most).astype(kind)


def setup_inputs(seed: int = 0, part: int = 0) -> dict:
    splits = jax.random.split(jax.random.key(seed), 8)
    part_keys = jax.random.split(jax.random.fold_in(splits[7], part), 8)
    hidden = bell_draw(part_keys[0], (STEPS, REQ, MODEL_WIDTH), 1.0, 6.0, ((1, 4), (2, 4)))
    request_adapter_keys = jax.random.split(jax.random.fold_in(part_keys[1], 1), REQ // ROWS_DEV)
    request_adapter_turns = jax.random.permutation(jax.random.fold_in(part_keys[1], 3), REQ // ROWS_DEV)
    request_adapter = jax.vmap(lambda own, number: shared_out(jax.random.fold_in(part_keys[1], 2), own, number, ROWS_DEV, ADAPTER_COUNT, 1, CAP, 2))(request_adapter_keys, request_adapter_turns).reshape((REQ, 1))
    adapter_row_index = jax.random.permutation(splits[2], ADAPTER_COUNT).astype(jnp.int32)
    adapter_scales = jnp.clip(jnp.exp(jax.random.uniform(splits[3], (ADAPTER_COUNT,), jnp.float32, math.log(0.5), math.log(2.0))), 0.5, 2.0)
    down_weight_rows = bell_draw(splits[4], (ADAPTER_COUNT, 2 * ADAPTER_RANK, MODEL_WIDTH), MODEL_WIDTH ** -0.5, 0.0625, ((0, 4), (2, 4)))
    query_up_weight = bell_draw(splits[5], (ADAPTER_COUNT, ADAPTER_RANK, QUERY_WIDTH), ADAPTER_RANK ** -0.5, 0.75, ((0, 4), (2, 4)))
    value_up_weight = bell_draw(splits[6], (ADAPTER_COUNT, ADAPTER_RANK, VALUE_WIDTH), ADAPTER_RANK ** -0.5, 0.75, ((0, 4), (2, 4)))
    return {"hidden": hidden, "request_adapter": request_adapter, "adapter_row_index": adapter_row_index, "adapter_scales": adapter_scales, "down_weight_rows": down_weight_rows, "query_up_weight": query_up_weight, "value_up_weight": value_up_weight}


def reference(hidden, request_adapter, adapter_row_index, adapter_scales, down_weight_rows, query_up_weight, value_up_weight):
    adapter_of = request_adapter[:, 0].astype(jnp.int32)
    total_rows = adapter_of.shape[0]
    most_rows = N_ROWS * CAP
    padded = jnp.concatenate([hidden, jnp.zeros((STEPS, 1, MODEL_WIDTH), jnp.bfloat16)], axis=1)
    start_q = jnp.zeros((STEPS, total_rows, QUERY_WIDTH), jnp.bfloat16)
    start_v = jnp.zeros((STEPS, total_rows, VALUE_WIDTH), jnp.bfloat16)

    def one_adapter(totals, adapter):
        out_q, out_v = totals
        holding_array = adapter_row_index[adapter].astype(jnp.int32)
        picked = jnp.nonzero(adapter_of == adapter, size=most_rows, fill_value=total_rows)[0].astype(jnp.int32)
        chosen = padded[:, picked, :].reshape(STEPS * most_rows, MODEL_WIDTH)
        down_weight = lax.dynamic_index_in_dim(down_weight_rows, holding_array, 0, keepdims=False)
        shrunk = jnp.dot(chosen, down_weight.T, preferred_element_type=jnp.float32)
        scaled = (shrunk * adapter_scales[adapter]).astype(jnp.bfloat16)
        query_weight = lax.dynamic_index_in_dim(query_up_weight, holding_array, 0, keepdims=False)
        value_weight = lax.dynamic_index_in_dim(value_up_weight, holding_array, 0, keepdims=False)
        part_q = jnp.dot(scaled[:, :ADAPTER_RANK], query_weight, preferred_element_type=jnp.float32).astype(jnp.bfloat16)
        part_v = jnp.dot(scaled[:, ADAPTER_RANK:], value_weight, preferred_element_type=jnp.float32).astype(jnp.bfloat16)
        out_q = out_q.at[:, picked, :].set(part_q.reshape(STEPS, most_rows, QUERY_WIDTH), mode="drop")
        out_v = out_v.at[:, picked, :].set(part_v.reshape(STEPS, most_rows, VALUE_WIDTH), mode="drop")
        return (out_q, out_v), None

    results, unused = lax.scan(one_adapter, (start_q, start_v), jnp.arange(ADAPTER_COUNT, dtype=jnp.int32))
    return results[0], results[1]
```

```python
import functools

import jax
import jax.numpy as jnp
from jax import lax
from jax.experimental import pallas as pl
from jax.experimental.pallas import tpu as pltpu
from jax.sharding import PartitionSpec as P

DOWN_CHUNKS = 2
UP_CHUNKS = 2
MESH = pl.DeviceIdType.MESH


def lora_kernel(
    holders,
    row_index_ref,
    scales_ref,
    adapter_ref,
    hidden_hbm,
    down_hbm,
    query_hbm,
    value_hbm,
    out_q_hbm,
    out_v_hbm,
    hidden_ref,
    down_all,
    query_all,
    value_all,
    acc_ref,
    core_buf,
    pair_sum,
    chip_buf,
    scaled_ref,
    target_ref,
    scale_ref,
    stage_q,
    stage_v,
    local_sem,
    z_send,
    z_recv,
    y_send,
    y_recv,
    h_send,
    h_recv,
    out_sem,
):
    steps, rows_here, cols = hidden_hbm.shape
    rank2 = down_hbm.shape[1]
    rank = query_hbm.shape[1]
    width_q = query_hbm.shape[2]
    group = lax.axis_index("groups")
    me = lax.axis_index("rows")
    head = lax.axis_index("heads")
    core = head % 2
    sibling = head + 1 - 2 * core
    across = (head + 2) % 4
    other_group = 1 - group
    half_d = rank2 // 2
    half_u = rank // 2
    chunk_d = half_d // DOWN_CHUNKS
    chunk_u = width_q // UP_CHUNKS
    pieces_d = [("d", c) for c in range(DOWN_CHUNKS)]
    pieces_u = [("v", 0)] + [("q", c) for c in range(UP_CHUNKS)]
    slot_of = {piece: at for at, piece in enumerate(pieces_d + pieces_u)}
    far = range(1, holders)

    def origin_of(way, dist):
        return me - dist if way == 0 else me + dist

    def exists(origin):
        return jnp.logical_and(origin >= 0, origin < holders)

    def view(ref, lead, piece, half):
        kind, c = piece
        if kind == "d":
            start = pl.multiple_of(half * half_d + c * chunk_d, 16)
            return ref.at[lead, pl.ds(start, chunk_d), :]
        start = pl.multiple_of(half * half_u, 16)
        if kind == "v":
            return ref.at[lead, pl.ds(start, half_u), :]
        return ref.at[lead, pl.ds(start, half_u), pl.ds(c * chunk_u, chunk_u)]

    own_of = {"d": down_hbm, "q": query_hbm, "v": value_hbm}
    all_of = {"d": down_all, "q": query_all, "v": value_all}

    def z_copy(way, dist, piece):
        origin = me - (dist - 1) if way == 0 else me + (dist - 1)
        to = me + 1 if way == 0 else me - 1
        dst = view(all_of[piece[0]], origin, piece, group)
        src = view(own_of[piece[0]], 0, piece, group) if dist == 1 else dst
        return pltpu.make_async_remote_copy(
            src_ref=src,
            dst_ref=dst,
            send_sem=z_send.at[way, dist - 1, slot_of[piece]],
            recv_sem=z_recv.at[way, dist - 1, slot_of[piece]],
            device_id={"rows": to},
            device_id_type=MESH,
        )

    def z_arrival(way, dist, piece):
        dst = view(all_of[piece[0]], origin_of(way, dist), piece, group)
        return pltpu.make_async_remote_copy(
            src_ref=dst,
            dst_ref=dst,
            send_sem=z_send.at[way, dist - 1, slot_of[piece]],
            recv_sem=z_recv.at[way, dist - 1, slot_of[piece]],
            device_id={"rows": me + 1 if way == 0 else me - 1},
            device_id_type=MESH,
        )

    def y_copy(way, dist, piece, half):
        ref = view(all_of[piece[0]], origin_of(way, dist), piece, half)
        return pltpu.make_async_remote_copy(
            src_ref=ref,
            dst_ref=ref,
            send_sem=y_send.at[way, dist - 1, slot_of[piece]],
            recv_sem=y_recv.at[way, dist - 1, slot_of[piece]],
            device_id={"groups": other_group},
            device_id_type=MESH,
        )

    def h_copy(stage, src, dst, to):
        return pltpu.make_async_remote_copy(
            src_ref=src,
            dst_ref=dst,
            send_sem=h_send.at[stage],
            recv_sem=h_recv.at[stage],
            device_id={"heads": to},
            device_id_type=MESH,
        )

    def next_exists(way):
        return me < holders - 1 if way == 0 else me > 0

    def start_own(pieces):
        for way in (0, 1):
            @pl.when(next_exists(way))
            def _():
                for piece in pieces:
                    z_copy(way, 1, piece).start()

    def take_z(dist, pieces):
        for piece in pieces:
            for way in (0, 1):
                @pl.when(exists(origin_of(way, dist)))
                def _():
                    z_arrival(way, dist, piece).wait_recv()
                    if dist < holders - 1:
                        @pl.when(next_exists(way))
                        def _():
                            z_copy(way, dist + 1, piece).start()
                    y_copy(way, dist, piece, group).start()

    def take_y(dist, pieces):
        for way in (0, 1):
            @pl.when(exists(origin_of(way, dist)))
            def _():
                for piece in pieces:
                    y_copy(way, dist, piece, other_group).wait_recv()

    local = [
        pltpu.make_async_copy(hidden_hbm, hidden_ref, local_sem.at[0]),
        pltpu.make_async_copy(down_hbm.at[0], down_all.at[me], local_sem.at[1]),
        pltpu.make_async_copy(query_hbm.at[0], query_all.at[me], local_sem.at[2]),
        pltpu.make_async_copy(value_hbm.at[0], value_all.at[me], local_sem.at[3]),
    ]
    for copy in local:
        copy.start()

    barrier = pltpu.get_barrier_semaphore()
    for way in (0, 1):
        @pl.when(next_exists(way))
        def _():
            pl.semaphore_signal(
                barrier, inc=1, device_id={"rows": me + 1 - 2 * way}, device_id_type=MESH
            )
    pl.semaphore_signal(barrier, inc=1, device_id={"groups": other_group}, device_id_type=MESH)
    for to in (sibling, across):
        pl.semaphore_signal(barrier, inc=1, device_id={"heads": to}, device_id_type=MESH)
    neighbours = (me > 0).astype(jnp.int32) + (me < holders - 1).astype(jnp.int32)
    pl.semaphore_wait(barrier, neighbours + 3)

    start_own(pieces_d)

    adapters = adapter_ref[...]
    target = jnp.zeros_like(adapters)
    scale = jnp.zeros(adapters.shape, jnp.float32)
    for a in range(row_index_ref.shape[0]):
        target = jnp.where(adapters == a, row_index_ref[a], target)
        scale = jnp.where(adapters == a, scales_ref[a], scale)
    target_ref[...] = jnp.broadcast_to(target, target_ref.shape)
    scale_ref[...] = jnp.broadcast_to(scale, scale_ref.shape)

    def shrink(origin, first=False):
        weight = down_all[origin]
        for step in range(steps):
            part = lax.dot_general(
                hidden_ref[step],
                weight,
                (((1,), (1,)), ((), ())),
                preferred_element_type=jnp.float32,
            )
            kept = 0.0 if first else acc_ref[step]
            acc_ref[step] = jnp.where(target_ref[...] == origin, part, kept)

    def shrink_far(dist):
        for way in (0, 1):
            @pl.when(exists(origin_of(way, dist)))
            def _():
                shrink(origin_of(way, dist))

    local[0].wait()
    local[1].wait()
    shrink(me, first=True)
    for dist in far:
        take_z(dist, pieces_d)
        if dist == max(1, holders - 2):
            start_own(pieces_u)
        if dist > 1:
            take_y(dist - 1, pieces_d)
            shrink_far(dist - 1)
    take_y(holders - 1, pieces_d)
    shrink_far(holders - 1)

    to_core = h_copy(0, acc_ref.at[1 - core], core_buf, sibling)
    to_chip = h_copy(1, pair_sum, chip_buf, across)
    to_core_back = h_copy(2, scaled_ref.at[core], scaled_ref.at[core], sibling)
    from_core_back = h_copy(2, scaled_ref.at[1 - core], scaled_ref.at[1 - core], sibling)

    to_core.start()
    take_z(1, pieces_u)
    to_core.wait_recv()
    pair_sum[...] = acc_ref[core] + core_buf[...]
    to_chip.start()
    for dist in range(2, holders - 1):
        take_z(dist, pieces_u)
    to_chip.wait_recv()
    scaled_ref[core] = ((pair_sum[...] + chip_buf[...]) * scale_ref[...]).astype(jnp.bfloat16)
    to_core_back.start()
    take_z(holders - 1, pieces_u)
    from_core_back.wait_recv()

    lane = lax.broadcasted_iota(jnp.int32, target_ref.shape, 1)
    low = lane < rank
    lefts = []
    for step in range(steps):
        both = scaled_ref[step].astype(jnp.float32)
        swapped = pltpu.roll(both, rank, 1)
        pair = []
        for doubled in (jnp.where(low, both, swapped), jnp.where(low, swapped, both)):
            blocks = []
            for k in range(holders // 2):
                mine = target_ref[...] == jnp.where(low, 2 * k, 2 * k + 1)
                blocks.append(jnp.where(mine, doubled, 0.0).astype(jnp.bfloat16))
            pair.append(jnp.concatenate(blocks, axis=1))
        lefts.append(pair)

    local[2].wait()
    local[3].wait()
    outs = []
    for piece in pieces_u:
        for dist in far:
            take_y(dist, [piece])
        at = pl.ds(0, value_all.shape[2]) if piece[0] == "v" else pl.ds(piece[1] * chunk_u, chunk_u)
        source, stage, out = (
            (value_all, stage_v, out_v_hbm) if piece[0] == "v" else (query_all, stage_q, out_q_hbm)
        )
        which = 1 if piece[0] == "v" else 0
        right = source[:, :, at]
        right = right.reshape(holders * rank, right.shape[2])
        for step in range(steps):
            stage[step, :, at] = jnp.dot(
                lefts[step][which], right, preferred_element_type=jnp.float32
            ).astype(jnp.bfloat16)
            copy = pltpu.make_async_copy(
                stage.at[step, :, at], out.at[step, :, at], out_sem.at[len(outs)]
            )
            copy.start()
            outs.append(copy)

    for pieces in (pieces_d, pieces_u):
        for dist in far:
            for way in (0, 1):
                origin = me - (dist - 1) if way == 0 else me + (dist - 1)

                @pl.when(jnp.logical_and(exists(origin), next_exists(way)))
                def _():
                    for piece in pieces:
                        z_copy(way, dist, piece).wait_send()

                @pl.when(exists(origin_of(way, dist)))
                def _():
                    for piece in pieces:
                        y_copy(way, dist, piece, group).wait_send()
    to_core.wait_send()
    to_chip.wait_send()
    to_core_back.wait_send()
    for copy in outs:
        copy.wait()


def per_device_weights(
    hidden,
    request_adapter,
    adapter_row_index,
    adapter_scales,
    down_weight_rows,
    query_up_weight,
    value_up_weight,
):
    steps, rows_here, cols = hidden.shape
    holders = lax.axis_size("rows")
    rank2 = down_weight_rows.shape[1]
    rank = query_up_weight.shape[1]
    width_q, width_v = query_up_weight.shape[2], value_up_weight.shape[2]
    slots = DOWN_CHUNKS + UP_CHUNKS + 1
    bf16, f32 = jnp.bfloat16, jnp.float32
    smem = pl.BlockSpec(memory_space=pltpu.SMEM)
    vmem = pl.BlockSpec(memory_space=pltpu.VMEM)
    anyw = pl.BlockSpec(memory_space=pl.ANY)
    return pl.pallas_call(
        functools.partial(lora_kernel, holders),
        out_shape=(
            jax.ShapeDtypeStruct((steps, rows_here, width_q), bf16),
            jax.ShapeDtypeStruct((steps, rows_here, width_v), bf16),
        ),
        in_specs=[smem, smem, vmem, anyw, anyw, anyw, anyw],
        out_specs=(anyw, anyw),
        scratch_shapes=[
            pltpu.VMEM((steps, rows_here, cols), bf16),
            pltpu.VMEM((holders, rank2, cols), bf16),
            pltpu.VMEM((holders, rank, width_q), bf16),
            pltpu.VMEM((holders, rank, width_v), bf16),
            pltpu.VMEM((steps, rows_here, rank2), f32),
            pltpu.VMEM((rows_here, rank2), f32),
            pltpu.VMEM((rows_here, rank2), f32),
            pltpu.VMEM((rows_here, rank2), f32),
            pltpu.VMEM((steps, rows_here, rank2), bf16),
            pltpu.VMEM((rows_here, rank2), jnp.int32),
            pltpu.VMEM((rows_here, rank2), f32),
            pltpu.VMEM((steps, rows_here, width_q), bf16),
            pltpu.VMEM((steps, rows_here, width_v), bf16),
            pltpu.SemaphoreType.DMA((4,)),
            pltpu.SemaphoreType.DMA((2, holders - 1, slots)),
            pltpu.SemaphoreType.DMA((2, holders - 1, slots)),
            pltpu.SemaphoreType.DMA((2, holders - 1, slots)),
            pltpu.SemaphoreType.DMA((2, holders - 1, slots)),
            pltpu.SemaphoreType.DMA((3,)),
            pltpu.SemaphoreType.DMA((3,)),
            pltpu.SemaphoreType.DMA((steps * (UP_CHUNKS + 1),)),
        ],
        compiler_params=pltpu.CompilerParams(
            collective_id=0, has_side_effects=True, vmem_limit_bytes=32 * 1024 * 1024
        ),
        name="lora_weights",
    )(
        adapter_row_index,
        adapter_scales,
        request_adapter,
        hidden,
        down_weight_rows,
        query_up_weight,
        value_up_weight,
    )


def shrink_rows(received, down_weight):
    flattened = received.reshape(-1, received.shape[-1])
    return lax.dot_general(
        flattened, down_weight, (((1,), (1,)), ((), ())), preferred_element_type=jnp.float32
    )


def expand_rows(summed, scale_value, query_weight, value_weight, shape_lead):
    rank_size = query_weight.shape[0]
    scaled = (summed * scale_value).astype(jnp.bfloat16)
    delta_q = jnp.dot(
        scaled[:, :rank_size], query_weight, preferred_element_type=jnp.float32
    ).astype(jnp.bfloat16)
    delta_v = jnp.dot(
        scaled[:, rank_size:], value_weight, preferred_element_type=jnp.float32
    ).astype(jnp.bfloat16)
    return (
        delta_q.reshape(shape_lead + (query_weight.shape[1],)),
        delta_v.reshape(shape_lead + (value_weight.shape[1],)),
    )


def per_device_rows(
    hidden,
    request_adapter,
    adapter_row_index,
    adapter_scales,
    down_weight_rows,
    query_up_weight,
    value_up_weight,
):
    step_count, rows_here, head_cols = hidden.shape
    holders = lax.axis_size("rows")
    capacity = 2 * rows_here // holders
    adapter_total = adapter_row_index.shape[0]
    down_weight = down_weight_rows[0]
    query_weight = query_up_weight[0]
    value_weight = value_up_weight[0]
    adapter_of = request_adapter[:, 0]
    listing = jnp.arange(adapter_total, dtype=jnp.int32)
    onehot = (adapter_of[:, None] == listing[None, :]).astype(jnp.int32)
    target = jnp.sum(onehot * adapter_row_index[None, :], axis=1)
    own_index = lax.axis_index("rows")
    own_scale = jnp.sum(jnp.where(adapter_row_index == own_index, adapter_scales, 0.0))
    earlier = jnp.cumsum(onehot, axis=0) - onehot
    position = jnp.sum(earlier * onehot, axis=1)
    slot_index = target * capacity + position

    def place_rows(rows_in):
        buffer = jnp.zeros((holders * capacity, head_cols), jnp.bfloat16)
        return buffer.at[slot_index].set(rows_in).reshape(holders, capacity, head_cols)

    def pick_back(returned):
        flattened = returned.reshape(holders * capacity, returned.shape[-1])
        return jnp.take(flattened, slot_index, axis=0)

    outgoing = jnp.stack(
        [place_rows(hidden[step_index]) for step_index in range(step_count)], axis=1
    )
    received = lax.all_to_all(outgoing, "rows", split_axis=0, concat_axis=0, tiled=True)
    summed = lax.psum(shrink_rows(received, down_weight), "heads")
    delta_q, delta_v = expand_rows(
        summed, own_scale, query_weight, value_weight, received.shape[:-1]
    )
    back_q = lax.all_to_all(delta_q, "rows", split_axis=0, concat_axis=0, tiled=True)
    back_v = lax.all_to_all(delta_v, "rows", split_axis=0, concat_axis=0, tiled=True)
    outs_q = [pick_back(back_q[:, step_index]) for step_index in range(step_count)]
    outs_v = [pick_back(back_v[:, step_index]) for step_index in range(step_count)]
    return (jnp.stack(outs_q), jnp.stack(outs_v))


def per_device(
    hidden,
    request_adapter,
    adapter_row_index,
    adapter_scales,
    down_weight_rows,
    query_up_weight,
    value_up_weight,
):
    steps, rows_here, cols = hidden.shape
    holders = lax.axis_size("rows")
    rank2 = down_weight_rows.shape[1]
    width = query_up_weight.shape[2] + value_up_weight.shape[2]
    by_weights = holders * (rank2 * cols + rank2 // 2 * width)
    by_rows = 2 * steps * rows_here * (cols + width)
    fits = (
        lax.axis_size("groups") == 2
        and lax.axis_size("heads") == 4
        and holders % 2 == 0
        and steps == 2
        and rank2 == 128
    )
    plan = per_device_weights if fits and by_weights < by_rows else per_device_rows
    return plan(
        hidden,
        request_adapter,
        adapter_row_index,
        adapter_scales,
        down_weight_rows,
        query_up_weight,
        value_up_weight,
    )


def solution(mesh):
    return jax.shard_map(
        per_device,
        mesh=mesh,
        in_specs=(
            P(None, ("groups", "rows"), "heads"),
            P(("groups", "rows"), None),
            P(),
            P(),
            P("rows", None, "heads"),
            P("rows", None, "heads"),
            P("rows", None, "heads"),
        ),
        out_specs=(P(None, ("groups", "rows"), "heads"), P(None, ("groups", "rows"), "heads")),
        check_vma=False,
    )
```

```python
import functools

import jax
import jax.numpy as jnp
from jax import lax
from jax.experimental import pallas as pl
from jax.experimental.pallas import tpu as pltpu
from jax.sharding import PartitionSpec as P

DOWN_CHUNKS = 4
UP_CHUNKS = 4
MESH = pl.DeviceIdType.MESH


def lora_kernel(
    holders,
    row_index_ref,
    scales_ref,
    adapter_ref,
    hidden_hbm,
    down_hbm,
    query_hbm,
    value_hbm,
    out_q_hbm,
    out_v_hbm,
    hidden_ref,
    down_all,
    query_all,
    value_all,
    acc_ref,
    core_buf,
    pair_sum,
    pair_out,
    chip_buf,
    scaled_ref,
    target_ref,
    scale_ref,
    stage_q,
    stage_v,
    local_sem,
    z_send,
    z_recv,
    y_send,
    y_recv,
    h_send,
    h_recv,
    out_sem,
):
    steps, rows_here, cols = hidden_hbm.shape
    rank2 = down_hbm.shape[1]
    rank = query_hbm.shape[1]
    width_q = query_hbm.shape[2]
    group = lax.axis_index("groups")
    me = lax.axis_index("rows")
    head = lax.axis_index("heads")
    core = head % 2
    sibling = head + 1 - 2 * core
    across = (head + 2) % 4
    other_group = 1 - group
    half_d = rank2 // 2
    half_u = rank // 2
    chunk_d = half_d // DOWN_CHUNKS
    chunk_u = width_q // UP_CHUNKS
    pieces_d = [("d", c) for c in range(DOWN_CHUNKS)]
    pieces_u = [("v", 0)] + [("q", c) for c in range(UP_CHUNKS)]
    slot_of = {piece: at for at, piece in enumerate(pieces_d + pieces_u)}
    far = range(1, holders)

    def origin_of(way, dist):
        return me - dist if way == 0 else me + dist

    def exists(origin):
        return jnp.logical_and(origin >= 0, origin < holders)

    def view(ref, lead, piece, half):
        kind, c = piece
        if kind == "d":
            start = pl.multiple_of(half * half_d + c * chunk_d, 16)
            return ref.at[lead, pl.ds(start, chunk_d), :]
        start = pl.multiple_of(half * half_u, 16)
        if kind == "v":
            return ref.at[lead, pl.ds(start, half_u), :]
        return ref.at[lead, pl.ds(start, half_u), pl.ds(c * chunk_u, chunk_u)]

    own_of = {"d": down_hbm, "q": query_hbm, "v": value_hbm}
    all_of = {"d": down_all, "q": query_all, "v": value_all}

    def z_copy(way, dist, piece):
        origin = me - (dist - 1) if way == 0 else me + (dist - 1)
        to = me + 1 if way == 0 else me - 1
        dst = view(all_of[piece[0]], origin, piece, group)
        src = view(own_of[piece[0]], 0, piece, group) if dist == 1 else dst
        return pltpu.make_async_remote_copy(
            src_ref=src,
            dst_ref=dst,
            send_sem=z_send.at[way, dist - 1, slot_of[piece]],
            recv_sem=z_recv.at[way, dist - 1, slot_of[piece]],
            device_id={"rows": to},
            device_id_type=MESH,
        )

    def z_arrival(way, dist, piece):
        dst = view(all_of[piece[0]], origin_of(way, dist), piece, group)
        return pltpu.make_async_remote_copy(
            src_ref=dst,
            dst_ref=dst,
            send_sem=z_send.at[way, dist - 1, slot_of[piece]],
            recv_sem=z_recv.at[way, dist - 1, slot_of[piece]],
            device_id={"rows": me + 1 if way == 0 else me - 1},
            device_id_type=MESH,
        )

    def y_copy(way, dist, piece, half):
        ref = view(all_of[piece[0]], origin_of(way, dist), piece, half)
        return pltpu.make_async_remote_copy(
            src_ref=ref,
            dst_ref=ref,
            send_sem=y_send.at[way, dist - 1, slot_of[piece]],
            recv_sem=y_recv.at[way, dist - 1, slot_of[piece]],
            device_id={"groups": other_group},
            device_id_type=MESH,
        )

    def h_copy(stage, src, dst, to):
        return pltpu.make_async_remote_copy(
            src_ref=src,
            dst_ref=dst,
            send_sem=h_send.at[stage],
            recv_sem=h_recv.at[stage],
            device_id={"heads": to},
            device_id_type=MESH,
        )

    def next_exists(way):
        return me < holders - 1 if way == 0 else me > 0

    def start_own(pieces):
        for way in (0, 1):
            @pl.when(next_exists(way))
            def _():
                for piece in pieces:
                    z_copy(way, 1, piece).start()

    def take_z(dist, pieces):
        for piece in pieces:
            for way in (0, 1):
                @pl.when(exists(origin_of(way, dist)))
                def _():
                    z_arrival(way, dist, piece).wait_recv()
                    if dist < holders - 1:
                        @pl.when(next_exists(way))
                        def _():
                            z_copy(way, dist + 1, piece).start()
                    y_copy(way, dist, piece, group).start()

    def take_y(dist, pieces):
        for way in (0, 1):
            @pl.when(exists(origin_of(way, dist)))
            def _():
                for piece in pieces:
                    y_copy(way, dist, piece, other_group).wait_recv()

    local = [
        pltpu.make_async_copy(hidden_hbm, hidden_ref, local_sem.at[0]),
        pltpu.make_async_copy(down_hbm.at[0], down_all.at[me], local_sem.at[1]),
        pltpu.make_async_copy(query_hbm.at[0], query_all.at[me], local_sem.at[2]),
        pltpu.make_async_copy(value_hbm.at[0], value_all.at[me], local_sem.at[3]),
    ]
    for copy in local:
        copy.start()

    barrier = pltpu.get_barrier_semaphore()
    for way in (0, 1):
        @pl.when(next_exists(way))
        def _():
            pl.semaphore_signal(
                barrier, inc=1, device_id={"rows": me + 1 - 2 * way}, device_id_type=MESH
            )
    pl.semaphore_signal(barrier, inc=1, device_id={"groups": other_group}, device_id_type=MESH)
    for to in (sibling, across):
        pl.semaphore_signal(barrier, inc=1, device_id={"heads": to}, device_id_type=MESH)
    neighbours = (me > 0).astype(jnp.int32) + (me < holders - 1).astype(jnp.int32)
    pl.semaphore_wait(barrier, neighbours + 3)

    start_own(pieces_d)

    adapters = adapter_ref[...]
    target = jnp.zeros_like(adapters)
    scale = jnp.zeros(adapters.shape, jnp.float32)
    for a in range(row_index_ref.shape[0]):
        target = jnp.where(adapters == a, row_index_ref[a], target)
        scale = jnp.where(adapters == a, scales_ref[a], scale)
    target_ref[...] = jnp.broadcast_to(target, target_ref.shape)
    scale_ref[...] = jnp.broadcast_to(scale, scale_ref.shape)

    def shrink(origin, first=False):
        weight = down_all[origin]
        for step in range(steps):
            part = lax.dot_general(
                hidden_ref[step],
                weight,
                (((1,), (1,)), ((), ())),
                preferred_element_type=jnp.float32,
            )
            kept = 0.0 if first else acc_ref[step]
            acc_ref[step] = jnp.where(target_ref[...] == origin, part, kept)

    def shrink_far(dist):
        for way in (0, 1):
            @pl.when(exists(origin_of(way, dist)))
            def _():
                shrink(origin_of(way, dist))

    local[0].wait()
    local[1].wait()
    shrink(me, first=True)
    for dist in far:
        take_z(dist, pieces_d)
        if dist == max(1, holders - 2):
            start_own(pieces_u)
        if dist > 1:
            take_y(dist - 1, pieces_d)
            shrink_far(dist - 1)
    take_y(holders - 1, pieces_d)
    shrink_far(holders - 1)

    to_core = h_copy(0, acc_ref.at[1 - core], core_buf, sibling)
    to_chip = h_copy(1, pair_out, chip_buf, across)
    to_core_back = h_copy(2, scaled_ref.at[core], scaled_ref.at[core], sibling)
    from_core_back = h_copy(2, scaled_ref.at[1 - core], scaled_ref.at[1 - core], sibling)

    to_core.start()
    take_z(1, pieces_u)
    to_core.wait_recv()
    pair_sum[...] = acc_ref[core] + core_buf[...]
    pair_out[...] = pair_sum[...].astype(jnp.bfloat16)
    to_chip.start()
    for dist in range(2, holders - 1):
        take_z(dist, pieces_u)
    to_chip.wait_recv()
    scaled_ref[core] = ((pair_sum[...] + chip_buf[...].astype(jnp.float32)) * scale_ref[...]).astype(jnp.bfloat16)
    to_core_back.start()
    take_z(holders - 1, pieces_u)
    from_core_back.wait_recv()

    lane = lax.broadcasted_iota(jnp.int32, target_ref.shape, 1)
    low = lane < rank
    lefts = []
    for step in range(steps):
        both = scaled_ref[step].astype(jnp.float32)
        swapped = pltpu.roll(both, rank, 1)
        pair = []
        for doubled in (jnp.where(low, both, swapped), jnp.where(low, swapped, both)):
            blocks = []
            for k in range(holders // 2):
                mine = target_ref[...] == jnp.where(low, 2 * k, 2 * k + 1)
                blocks.append(jnp.where(mine, doubled, 0.0).astype(jnp.bfloat16))
            pair.append(jnp.concatenate(blocks, axis=1))
        lefts.append(pair)

    local[2].wait()
    local[3].wait()
    outs = []
    for piece in pieces_u:
        for dist in far:
            take_y(dist, [piece])
        at = pl.ds(0, value_all.shape[2]) if piece[0] == "v" else pl.ds(piece[1] * chunk_u, chunk_u)
        source, stage, out = (
            (value_all, stage_v, out_v_hbm) if piece[0] == "v" else (query_all, stage_q, out_q_hbm)
        )
        which = 1 if piece[0] == "v" else 0
        right = source[:, :, at]
        right = right.reshape(holders * rank, right.shape[2])
        for step in range(steps):
            stage[step, :, at] = jnp.dot(
                lefts[step][which], right, preferred_element_type=jnp.float32
            ).astype(jnp.bfloat16)
            copy = pltpu.make_async_copy(
                stage.at[step, :, at], out.at[step, :, at], out_sem.at[len(outs)]
            )
            copy.start()
            outs.append(copy)

    for pieces in (pieces_d, pieces_u):
        for dist in far:
            for way in (0, 1):
                origin = me - (dist - 1) if way == 0 else me + (dist - 1)

                @pl.when(jnp.logical_and(exists(origin), next_exists(way)))
                def _():
                    for piece in pieces:
                        z_copy(way, dist, piece).wait_send()

                @pl.when(exists(origin_of(way, dist)))
                def _():
                    for piece in pieces:
                        y_copy(way, dist, piece, group).wait_send()
    to_core.wait_send()
    to_chip.wait_send()
    to_core_back.wait_send()
    for copy in outs:
        copy.wait()


def per_device_weights(
    hidden,
    request_adapter,
    adapter_row_index,
    adapter_scales,
    down_weight_rows,
    query_up_weight,
    value_up_weight,
):
    steps, rows_here, cols = hidden.shape
    holders = lax.axis_size("rows")
    rank2 = down_weight_rows.shape[1]
    rank = query_up_weight.shape[1]
    width_q, width_v = query_up_weight.shape[2], value_up_weight.shape[2]
    slots = DOWN_CHUNKS + UP_CHUNKS + 1
    bf16, f32 = jnp.bfloat16, jnp.float32
    smem = pl.BlockSpec(memory_space=pltpu.SMEM)
    vmem = pl.BlockSpec(memory_space=pltpu.VMEM)
    anyw = pl.BlockSpec(memory_space=pl.ANY)
    return pl.pallas_call(
        functools.partial(lora_kernel, holders),
        out_shape=(
            jax.ShapeDtypeStruct((steps, rows_here, width_q), bf16),
            jax.ShapeDtypeStruct((steps, rows_here, width_v), bf16),
        ),
        in_specs=[smem, smem, vmem, anyw, anyw, anyw, anyw],
        out_specs=(anyw, anyw),
        scratch_shapes=[
            pltpu.VMEM((steps, rows_here, cols), bf16),
            pltpu.VMEM((holders, rank2, cols), bf16),
            pltpu.VMEM((holders, rank, width_q), bf16),
            pltpu.VMEM((holders, rank, width_v), bf16),
            pltpu.VMEM((steps, rows_here, rank2), f32),
            pltpu.VMEM((rows_here, rank2), f32),
            pltpu.VMEM((rows_here, rank2), f32),
            pltpu.VMEM((rows_here, rank2), bf16),
            pltpu.VMEM((rows_here, rank2), bf16),
            pltpu.VMEM((steps, rows_here, rank2), bf16),
            pltpu.VMEM((rows_here, rank2), jnp.int32),
            pltpu.VMEM((rows_here, rank2), f32),
            pltpu.VMEM((steps, rows_here, width_q), bf16),
            pltpu.VMEM((steps, rows_here, width_v), bf16),
            pltpu.SemaphoreType.DMA((4,)),
            pltpu.SemaphoreType.DMA((2, holders - 1, slots)),
            pltpu.SemaphoreType.DMA((2, holders - 1, slots)),
            pltpu.SemaphoreType.DMA((2, holders - 1, slots)),
            pltpu.SemaphoreType.DMA((2, holders - 1, slots)),
            pltpu.SemaphoreType.DMA((3,)),
            pltpu.SemaphoreType.DMA((3,)),
            pltpu.SemaphoreType.DMA((steps * (UP_CHUNKS + 1),)),
        ],
        compiler_params=pltpu.CompilerParams(
            collective_id=0, has_side_effects=True, vmem_limit_bytes=60 * 1024 * 1024
        ),
        name="lora_weights",
    )(
        adapter_row_index,
        adapter_scales,
        request_adapter,
        hidden,
        down_weight_rows,
        query_up_weight,
        value_up_weight,
    )


def shrink_rows(received, down_weight):
    flattened = received.reshape(-1, received.shape[-1])
    return lax.dot_general(
        flattened, down_weight, (((1,), (1,)), ((), ())), preferred_element_type=jnp.float32
    )


def expand_rows(summed, scale_value, query_weight, value_weight, shape_lead):
    rank_size = query_weight.shape[0]
    scaled = (summed * scale_value).astype(jnp.bfloat16)
    delta_q = jnp.dot(
        scaled[:, :rank_size], query_weight, preferred_element_type=jnp.float32
    ).astype(jnp.bfloat16)
    delta_v = jnp.dot(
        scaled[:, rank_size:], value_weight, preferred_element_type=jnp.float32
    ).astype(jnp.bfloat16)
    return (
        delta_q.reshape(shape_lead + (query_weight.shape[1],)),
        delta_v.reshape(shape_lead + (value_weight.shape[1],)),
    )


def per_device_rows(
    hidden,
    request_adapter,
    adapter_row_index,
    adapter_scales,
    down_weight_rows,
    query_up_weight,
    value_up_weight,
):
    step_count, rows_here, head_cols = hidden.shape
    holders = lax.axis_size("rows")
    capacity = 2 * rows_here // holders
    adapter_total = adapter_row_index.shape[0]
    down_weight = down_weight_rows[0]
    query_weight = query_up_weight[0]
    value_weight = value_up_weight[0]
    adapter_of = request_adapter[:, 0]
    listing = jnp.arange(adapter_total, dtype=jnp.int32)
    onehot = (adapter_of[:, None] == listing[None, :]).astype(jnp.int32)
    target = jnp.sum(onehot * adapter_row_index[None, :], axis=1)
    own_index = lax.axis_index("rows")
    own_scale = jnp.sum(jnp.where(adapter_row_index == own_index, adapter_scales, 0.0))
    earlier = jnp.cumsum(onehot, axis=0) - onehot
    position = jnp.sum(earlier * onehot, axis=1)
    slot_index = target * capacity + position

    def place_rows(rows_in):
        buffer = jnp.zeros((holders * capacity, head_cols), jnp.bfloat16)
        return buffer.at[slot_index].set(rows_in).reshape(holders, capacity, head_cols)

    def pick_back(returned):
        flattened = returned.reshape(holders * capacity, returned.shape[-1])
        return jnp.take(flattened, slot_index, axis=0)

    outgoing = jnp.stack(
        [place_rows(hidden[step_index]) for step_index in range(step_count)], axis=1
    )
    received = lax.all_to_all(outgoing, "rows", split_axis=0, concat_axis=0, tiled=True)
    summed = lax.psum(shrink_rows(received, down_weight), "heads")
    delta_q, delta_v = expand_rows(
        summed, own_scale, query_weight, value_weight, received.shape[:-1]
    )
    back_q = lax.all_to_all(delta_q, "rows", split_axis=0, concat_axis=0, tiled=True)
    back_v = lax.all_to_all(delta_v, "rows", split_axis=0, concat_axis=0, tiled=True)
    outs_q = [pick_back(back_q[:, step_index]) for step_index in range(step_count)]
    outs_v = [pick_back(back_v[:, step_index]) for step_index in range(step_count)]
    return (jnp.stack(outs_q), jnp.stack(outs_v))


def per_device(
    hidden,
    request_adapter,
    adapter_row_index,
    adapter_scales,
    down_weight_rows,
    query_up_weight,
    value_up_weight,
):
    steps, rows_here, cols = hidden.shape
    holders = lax.axis_size("rows")
    rank2 = down_weight_rows.shape[1]
    width = query_up_weight.shape[2] + value_up_weight.shape[2]
    by_weights = holders * (rank2 * cols + rank2 // 2 * width)
    by_rows = 2 * steps * rows_here * (cols + width)
    fits = (
        lax.axis_size("groups") == 2
        and lax.axis_size("heads") == 4
        and holders % 2 == 0
        and steps == 2
        and rank2 == 128
    )
    plan = per_device_weights if fits and by_weights < by_rows else per_device_rows
    return plan(
        hidden,
        request_adapter,
        adapter_row_index,
        adapter_scales,
        down_weight_rows,
        query_up_weight,
        value_up_weight,
    )


def solution(mesh):
    return jax.shard_map(
        per_device,
        mesh=mesh,
        in_specs=(
            P(None, ("groups", "rows"), "heads"),
            P(("groups", "rows"), None),
            P(),
            P(),
            P("rows", None, "heads"),
            P("rows", None, "heads"),
            P("rows", None, "heads"),
        ),
        out_specs=(P(None, ("groups", "rows"), "heads"), P(None, ("groups", "rows"), "heads")),
        check_vma=False,
    )
```

```python
import functools

import jax
import jax.numpy as jnp
from jax import lax
from jax.experimental import pallas as pl
from jax.experimental.pallas import tpu as pltpu
from jax.sharding import PartitionSpec as P

DOWN_CHUNKS = 4
UP_CHUNKS = 2
MESH = pl.DeviceIdType.MESH


def lora_kernel(
    holders,
    row_index_ref,
    scales_ref,
    adapter_ref,
    hidden_hbm,
    down_hbm,
    query_hbm,
    value_hbm,
    out_q_hbm,
    out_v_hbm,
    hidden_ref,
    down_all,
    query_all,
    value_all,
    acc_ref,
    core_buf,
    pair_sum,
    chip_buf,
    scaled_ref,
    target_ref,
    scale_ref,
    stage_q,
    stage_v,
    local_sem,
    z_send,
    z_recv,
    y_send,
    y_recv,
    h_send,
    h_recv,
    out_sem,
):
    steps, rows_here, cols = hidden_hbm.shape
    rank2 = down_hbm.shape[1]
    rank = query_hbm.shape[1]
    width_q = query_hbm.shape[2]
    group = lax.axis_index("groups")
    me = lax.axis_index("rows")
    head = lax.axis_index("heads")
    core = head % 2
    sibling = head + 1 - 2 * core
    across = (head + 2) % 4
    other_group = 1 - group
    half_d = rank2 // 2
    half_u = rank // 2
    chunk_d = half_d // DOWN_CHUNKS
    chunk_u = width_q // UP_CHUNKS
    pieces_d = [("d", c) for c in range(DOWN_CHUNKS)]
    pieces_u = [("v", 0)] + [("q", c) for c in range(UP_CHUNKS)]
    slot_of = {piece: at for at, piece in enumerate(pieces_d + pieces_u)}
    far = range(1, holders)

    def origin_of(way, dist):
        return me - dist if way == 0 else me + dist

    def exists(origin):
        return jnp.logical_and(origin >= 0, origin < holders)

    def view(ref, lead, piece, half):
        kind, c = piece
        if kind == "d":
            start = pl.multiple_of(half * half_d + c * chunk_d, 16)
            return ref.at[lead, pl.ds(start, chunk_d), :]
        start = pl.multiple_of(half * half_u, 16)
        if kind == "v":
            return ref.at[lead, pl.ds(start, half_u), :]
        return ref.at[lead, pl.ds(start, half_u), pl.ds(c * chunk_u, chunk_u)]

    own_of = {"d": down_hbm, "q": query_hbm, "v": value_hbm}
    all_of = {"d": down_all, "q": query_all, "v": value_all}

    def z_copy(way, dist, piece):
        origin = me - (dist - 1) if way == 0 else me + (dist - 1)
        to = me + 1 if way == 0 else me - 1
        dst = view(all_of[piece[0]], origin, piece, group)
        src = view(own_of[piece[0]], 0, piece, group) if dist == 1 else dst
        return pltpu.make_async_remote_copy(
            src_ref=src,
            dst_ref=dst,
            send_sem=z_send.at[way, dist - 1, slot_of[piece]],
            recv_sem=z_recv.at[way, dist - 1, slot_of[piece]],
            device_id={"rows": to},
            device_id_type=MESH,
        )

    def z_arrival(way, dist, piece):
        dst = view(all_of[piece[0]], origin_of(way, dist), piece, group)
        return pltpu.make_async_remote_copy(
            src_ref=dst,
            dst_ref=dst,
            send_sem=z_send.at[way, dist - 1, slot_of[piece]],
            recv_sem=z_recv.at[way, dist - 1, slot_of[piece]],
            device_id={"rows": me + 1 if way == 0 else me - 1},
            device_id_type=MESH,
        )

    def y_copy(way, dist, piece, half):
        ref = view(all_of[piece[0]], origin_of(way, dist), piece, half)
        return pltpu.make_async_remote_copy(
            src_ref=ref,
            dst_ref=ref,
            send_sem=y_send.at[way, dist - 1, slot_of[piece]],
            recv_sem=y_recv.at[way, dist - 1, slot_of[piece]],
            device_id={"groups": other_group},
            device_id_type=MESH,
        )

    def h_copy(stage, src, dst, to):
        return pltpu.make_async_remote_copy(
            src_ref=src,
            dst_ref=dst,
            send_sem=h_send.at[stage],
            recv_sem=h_recv.at[stage],
            device_id={"heads": to},
            device_id_type=MESH,
        )

    def next_exists(way):
        return me < holders - 1 if way == 0 else me > 0

    def start_own(pieces):
        for way in (0, 1):
            @pl.when(next_exists(way))
            def _():
                for piece in pieces:
                    z_copy(way, 1, piece).start()

    def take_z(dist, pieces):
        for piece in pieces:
            for way in (0, 1):
                @pl.when(exists(origin_of(way, dist)))
                def _():
                    z_arrival(way, dist, piece).wait_recv()
                    if dist < holders - 1:
                        @pl.when(next_exists(way))
                        def _():
                            z_copy(way, dist + 1, piece).start()
                    y_copy(way, dist, piece, group).start()

    def take_y(dist, pieces):
        for way in (0, 1):
            @pl.when(exists(origin_of(way, dist)))
            def _():
                for piece in pieces:
                    y_copy(way, dist, piece, other_group).wait_recv()

    local = [
        pltpu.make_async_copy(hidden_hbm, hidden_ref, local_sem.at[0]),
        pltpu.make_async_copy(down_hbm.at[0], down_all.at[me], local_sem.at[1]),
        pltpu.make_async_copy(query_hbm.at[0], query_all.at[me], local_sem.at[2]),
        pltpu.make_async_copy(value_hbm.at[0], value_all.at[me], local_sem.at[3]),
    ]
    for copy in local:
        copy.start()

    barrier = pltpu.get_barrier_semaphore()
    for way in (0, 1):
        @pl.when(next_exists(way))
        def _():
            pl.semaphore_signal(
                barrier, inc=1, device_id={"rows": me + 1 - 2 * way}, device_id_type=MESH
            )
    pl.semaphore_signal(barrier, inc=1, device_id={"groups": other_group}, device_id_type=MESH)
    for to in (sibling, across):
        pl.semaphore_signal(barrier, inc=1, device_id={"heads": to}, device_id_type=MESH)
    neighbours = (me > 0).astype(jnp.int32) + (me < holders - 1).astype(jnp.int32)
    pl.semaphore_wait(barrier, neighbours + 3)

    start_own(pieces_d)

    adapters = adapter_ref[...]
    target = jnp.zeros_like(adapters)
    scale = jnp.zeros(adapters.shape, jnp.float32)
    for a in range(row_index_ref.shape[0]):
        target = jnp.where(adapters == a, row_index_ref[a], target)
        scale = jnp.where(adapters == a, scales_ref[a], scale)
    spread = (rank2, rows_here)
    target_ref[...] = jnp.broadcast_to(target.astype(jnp.float32), spread).T.astype(jnp.int32)
    scale_ref[...] = jnp.broadcast_to(scale, spread).T

    def shrink(origin, first=False):
        weight = down_all[origin]
        for step in range(steps):
            part = lax.dot_general(
                hidden_ref[step],
                weight,
                (((1,), (1,)), ((), ())),
                preferred_element_type=jnp.float32,
            )
            kept = 0.0 if first else acc_ref[step]
            acc_ref[step] = jnp.where(target_ref[...] == origin, part, kept)

    def shrink_far(dist):
        for way in (0, 1):
            @pl.when(exists(origin_of(way, dist)))
            def _():
                shrink(origin_of(way, dist))

    local[0].wait()
    local[1].wait()
    shrink(me, first=True)
    for dist in far:
        take_z(dist, pieces_d)
        if dist == max(1, holders - 2):
            start_own(pieces_u)
        if dist > 1:
            take_y(dist - 1, pieces_d)
            shrink_far(dist - 1)
    take_y(holders - 1, pieces_d)
    shrink_far(holders - 1)

    to_core = h_copy(0, acc_ref.at[1 - core], core_buf, sibling)
    to_chip = h_copy(1, pair_sum, chip_buf, across)
    to_core_back = h_copy(2, scaled_ref.at[core], scaled_ref.at[core], sibling)
    from_core_back = h_copy(2, scaled_ref.at[1 - core], scaled_ref.at[1 - core], sibling)

    to_core.start()
    take_z(1, pieces_u)
    to_core.wait_recv()
    pair_sum[...] = acc_ref[core] + core_buf[...]
    to_chip.start()
    for dist in range(2, holders - 1):
        take_z(dist, pieces_u)
    to_chip.wait_recv()
    scaled_ref[core] = ((pair_sum[...] + chip_buf[...]) * scale_ref[...]).astype(jnp.bfloat16)
    to_core_back.start()
    take_z(holders - 1, pieces_u)
    from_core_back.wait_recv()

    lane = lax.broadcasted_iota(jnp.int32, target_ref.shape, 1)
    low = lane < rank
    lefts = []
    for step in range(steps):
        both = scaled_ref[step].astype(jnp.float32)
        swapped = pltpu.roll(both, rank, 1)
        pair = []
        for doubled in (jnp.where(low, both, swapped), jnp.where(low, swapped, both)):
            blocks = []
            for k in range(holders // 2):
                mine = target_ref[...] == jnp.where(low, 2 * k, 2 * k + 1)
                blocks.append(jnp.where(mine, doubled, 0.0).astype(jnp.bfloat16))
            pair.append(jnp.concatenate(blocks, axis=1))
        lefts.append(pair)

    local[2].wait()
    local[3].wait()
    outs = []
    for piece in pieces_u:
        for dist in far:
            take_y(dist, [piece])
        at = pl.ds(0, value_all.shape[2]) if piece[0] == "v" else pl.ds(piece[1] * chunk_u, chunk_u)
        source, stage, out = (
            (value_all, stage_v, out_v_hbm) if piece[0] == "v" else (query_all, stage_q, out_q_hbm)
        )
        which = 1 if piece[0] == "v" else 0
        right = source[:, :, at]
        right = right.reshape(holders * rank, right.shape[2])
        for step in range(steps):
            stage[step, :, at] = jnp.dot(
                lefts[step][which], right, preferred_element_type=jnp.float32
            ).astype(jnp.bfloat16)
            copy = pltpu.make_async_copy(
                stage.at[step, :, at], out.at[step, :, at], out_sem.at[len(outs)]
            )
            copy.start()
            outs.append(copy)

    for pieces in (pieces_d, pieces_u):
        for dist in far:
            for way in (0, 1):
                origin = me - (dist - 1) if way == 0 else me + (dist - 1)

                @pl.when(jnp.logical_and(exists(origin), next_exists(way)))
                def _():
                    for piece in pieces:
                        z_copy(way, dist, piece).wait_send()

                @pl.when(exists(origin_of(way, dist)))
                def _():
                    for piece in pieces:
                        y_copy(way, dist, piece, group).wait_send()
    to_core.wait_send()
    to_chip.wait_send()
    to_core_back.wait_send()
    for copy in outs:
        copy.wait()


def per_device_weights(
    hidden,
    request_adapter,
    adapter_row_index,
    adapter_scales,
    down_weight_rows,
    query_up_weight,
    value_up_weight,
):
    steps, rows_here, cols = hidden.shape
    holders = lax.axis_size("rows")
    rank2 = down_weight_rows.shape[1]
    rank = query_up_weight.shape[1]
    width_q, width_v = query_up_weight.shape[2], value_up_weight.shape[2]
    slots = DOWN_CHUNKS + UP_CHUNKS + 1
    bf16, f32 = jnp.bfloat16, jnp.float32
    smem = pl.BlockSpec(memory_space=pltpu.SMEM)
    vmem = pl.BlockSpec(memory_space=pltpu.VMEM)
    anyw = pl.BlockSpec(memory_space=pl.ANY)
    return pl.pallas_call(
        functools.partial(lora_kernel, holders),
        out_shape=(
            jax.ShapeDtypeStruct((steps, rows_here, width_q), bf16),
            jax.ShapeDtypeStruct((steps, rows_here, width_v), bf16),
        ),
        in_specs=[smem, smem, vmem, anyw, anyw, anyw, anyw],
        out_specs=(anyw, anyw),
        scratch_shapes=[
            pltpu.VMEM((steps, rows_here, cols), bf16),
            pltpu.VMEM((holders, rank2, cols), bf16),
            pltpu.VMEM((holders, rank, width_q), bf16),
            pltpu.VMEM((holders, rank, width_v), bf16),
            pltpu.VMEM((steps, rows_here, rank2), f32),
            pltpu.VMEM((rows_here, rank2), f32),
            pltpu.VMEM((rows_here, rank2), f32),
            pltpu.VMEM((rows_here, rank2), f32),
            pltpu.VMEM((steps, rows_here, rank2), bf16),
            pltpu.VMEM((rows_here, rank2), jnp.int32),
            pltpu.VMEM((rows_here, rank2), f32),
            pltpu.VMEM((steps, rows_here, width_q), bf16),
            pltpu.VMEM((steps, rows_here, width_v), bf16),
            pltpu.SemaphoreType.DMA((4,)),
            pltpu.SemaphoreType.DMA((2, holders - 1, slots)),
            pltpu.SemaphoreType.DMA((2, holders - 1, slots)),
            pltpu.SemaphoreType.DMA((2, holders - 1, slots)),
            pltpu.SemaphoreType.DMA((2, holders - 1, slots)),
            pltpu.SemaphoreType.DMA((3,)),
            pltpu.SemaphoreType.DMA((3,)),
            pltpu.SemaphoreType.DMA((steps * (UP_CHUNKS + 1),)),
        ],
        compiler_params=pltpu.CompilerParams(
            collective_id=0, has_side_effects=True, vmem_limit_bytes=60 * 1024 * 1024
        ),
        name="lora_weights",
    )(
        adapter_row_index,
        adapter_scales,
        request_adapter.reshape(1, rows_here),
        hidden,
        down_weight_rows,
        query_up_weight,
        value_up_weight,
    )


def shrink_rows(received, down_weight):
    flattened = received.reshape(-1, received.shape[-1])
    return lax.dot_general(
        flattened, down_weight, (((1,), (1,)), ((), ())), preferred_element_type=jnp.float32
    )


def expand_rows(summed, scale_value, query_weight, value_weight, shape_lead):
    rank_size = query_weight.shape[0]
    scaled = (summed * scale_value).astype(jnp.bfloat16)
    delta_q = jnp.dot(
        scaled[:, :rank_size], query_weight, preferred_element_type=jnp.float32
    ).astype(jnp.bfloat16)
    delta_v = jnp.dot(
        scaled[:, rank_size:], value_weight, preferred_element_type=jnp.float32
    ).astype(jnp.bfloat16)
    return (
        delta_q.reshape(shape_lead + (query_weight.shape[1],)),
        delta_v.reshape(shape_lead + (value_weight.shape[1],)),
    )


def per_device_rows(
    hidden,
    request_adapter,
    adapter_row_index,
    adapter_scales,
    down_weight_rows,
    query_up_weight,
    value_up_weight,
):
    step_count, rows_here, head_cols = hidden.shape
    holders = lax.axis_size("rows")
    capacity = 2 * rows_here // holders
    adapter_total = adapter_row_index.shape[0]
    down_weight = down_weight_rows[0]
    query_weight = query_up_weight[0]
    value_weight = value_up_weight[0]
    adapter_of = request_adapter[:, 0]
    listing = jnp.arange(adapter_total, dtype=jnp.int32)
    onehot = (adapter_of[:, None] == listing[None, :]).astype(jnp.int32)
    target = jnp.sum(onehot * adapter_row_index[None, :], axis=1)
    own_index = lax.axis_index("rows")
    own_scale = jnp.sum(jnp.where(adapter_row_index == own_index, adapter_scales, 0.0))
    earlier = jnp.cumsum(onehot, axis=0) - onehot
    position = jnp.sum(earlier * onehot, axis=1)
    slot_index = target * capacity + position

    def place_rows(rows_in):
        buffer = jnp.zeros((holders * capacity, head_cols), jnp.bfloat16)
        return buffer.at[slot_index].set(rows_in).reshape(holders, capacity, head_cols)

    def pick_back(returned):
        flattened = returned.reshape(holders * capacity, returned.shape[-1])
        return jnp.take(flattened, slot_index, axis=0)

    outgoing = jnp.stack(
        [place_rows(hidden[step_index]) for step_index in range(step_count)], axis=1
    )
    received = lax.all_to_all(outgoing, "rows", split_axis=0, concat_axis=0, tiled=True)
    summed = lax.psum(shrink_rows(received, down_weight), "heads")
    delta_q, delta_v = expand_rows(
        summed, own_scale, query_weight, value_weight, received.shape[:-1]
    )
    back_q = lax.all_to_all(delta_q, "rows", split_axis=0, concat_axis=0, tiled=True)
    back_v = lax.all_to_all(delta_v, "rows", split_axis=0, concat_axis=0, tiled=True)
    outs_q = [pick_back(back_q[:, step_index]) for step_index in range(step_count)]
    outs_v = [pick_back(back_v[:, step_index]) for step_index in range(step_count)]
    return (jnp.stack(outs_q), jnp.stack(outs_v))


def per_device(
    hidden,
    request_adapter,
    adapter_row_index,
    adapter_scales,
    down_weight_rows,
    query_up_weight,
    value_up_weight,
):
    steps, rows_here, cols = hidden.shape
    holders = lax.axis_size("rows")
    rank2 = down_weight_rows.shape[1]
    width = query_up_weight.shape[2] + value_up_weight.shape[2]
    by_weights = holders * (rank2 * cols + rank2 // 2 * width)
    by_rows = 2 * steps * rows_here * (cols + width)
    fits = (
        lax.axis_size("groups") == 2
        and lax.axis_size("heads") == 4
        and holders % 2 == 0
        and steps == 2
        and rank2 == 128
    )
    plan = per_device_weights if fits and by_weights < by_rows else per_device_rows
    return plan(
        hidden,
        request_adapter,
        adapter_row_index,
        adapter_scales,
        down_weight_rows,
        query_up_weight,
        value_up_weight,
    )


def solution(mesh):
    return jax.shard_map(
        per_device,
        mesh=mesh,
        in_specs=(
            P(None, ("groups", "rows"), "heads"),
            P(("groups", "rows"), None),
            P(),
            P(),
            P("rows", None, "heads"),
            P("rows", None, "heads"),
            P("rows", None, "heads"),
        ),
        out_specs=(P(None, ("groups", "rows"), "heads"), P(None, ("groups", "rows"), "heads")),
        check_vma=False,
    )
```
